32 devices in a mesh: groups: 2 (over x), chan: 8 (over z, y), quad: 2 (over core).
Axes of the slice: x: 2, y: 2, z: 4, core: 2. Of those that a mesh axis runs over, the one named last changes fastest.
Arguments:
- voltages: bfloat16 [4, 256, 265216], P(('groups', 'quad'), 'chan'), parts along dimension 0, may hold values from -6 to 6
- filter_taps: float32 [4, 1024], replicated, may hold values from -0.5 to 1.5
Outputs:
- visibilities: float32 [1024, 2, 256, 512], P(('groups', 'chan'), 'quad'), parts along dimension 0
The draws below stay inside these ranges and needn't reach their ends.
There are 2 independent parts, one for each index of `groups`. The reference program is written for one: setup_inputs(seed, part) draws one part's arguments, and reference() takes and returns one part's arrays. A program takes and returns all parts, laid end to end along the dimension named above; an argument that names none is the same for every part. Nothing has to cross between parts.
All inputs are finite; a program needn't handle non-finite values.
Results may differ from the reference program's by a relative error of at most 0.0047.
Values may be sent and summed in bfloat16 or wider, within the bound.
A program may use at most 320 MiB of HBM per device.

```python
import math
import jax
import jax.numpy as jnp
from jax import lax

TILES = 256
POINTS = 1024
TAPS = 4
SPECTRA = 256
FINE = 512
SAMPLES = 265216


def draw_filter_taps(key, part):
    key = jax.random.fold_in(key, 7)
    length = TAPS * POINTS
    offsets = (jnp.arange(length, dtype=jnp.float32) - length / 2 + 0.5) / POINTS
    prototype = jnp.sinc(offsets)
    factors = jax.random.uniform(key, (length,), jnp.float32, 0.6, 1.4)
    return (prototype * factors).reshape(TAPS, POINTS)


def block_scale(rng, extent, shards, low, largest):
    level = 1.0
    for dim, blocks in shards:
        draws = jax.random.uniform(jax.random.fold_in(jax.random.fold_in(rng, 6), dim), (blocks,), jnp.float32, low / len(shards), largest / len(shards))
        level = level * jnp.repeat(jnp.exp(draws), extent[dim] // blocks).reshape((-1,) + (1,) * (len(extent) - 1 - dim))
    return level


def centred(rng, shape, deviation, reach, shards=(), kind=jnp.bfloat16):
    gain = block_scale(rng, shape, shards, -0.22, 0.18) if shards else 1.0
    values = jax.random.normal(rng, shape, jnp.float32) * deviation * gain
    return jnp.minimum(jnp.maximum(values, -reach), reach).astype(kind)


def setup_inputs(seed: int = 0, part: int = 0) -> dict:
    arg_keys = jax.random.split(jax.random.key(seed), 3)
    part_splits = jax.random.split(jax.random.fold_in(arg_keys[2], part), 3)
    return {
        "voltages": centred(part_splits[0], (2, TILES, SAMPLES), 1.0, 6.0, ((0, 2), (1, 8))),
        "filter_taps": draw_filter_taps(jax.random.fold_in(arg_keys[2], 71), part),
    }


def phase_table(points):
    column = jnp.arange(points, dtype=jnp.int32)
    channel = jnp.arange(points // 2, dtype=jnp.int32)
    turns = channel[:, None] * column[None, :] % points
    angles = turns.astype(jnp.float32) * jnp.float32(2.0 * math.pi / points)
    weight = jnp.float32(1.0 / math.sqrt(points))
    return jnp.concatenate([jnp.cos(angles) * weight, -jnp.sin(angles) * weight], axis=0).astype(jnp.bfloat16)

def reference(voltages, filter_taps):
    inputs = voltages.reshape(2 * TILES, SPECTRA + TAPS - 1, POINTS)
    table_wide = phase_table(POINTS).astype(jnp.float32)

    def channelize(frames):
        filtered = jnp.zeros((SPECTRA, POINTS), jnp.float32)
        for tap_index in range(TAPS):
            filtered = filtered + frames[tap_index:tap_index + SPECTRA].astype(jnp.float32) * filter_taps[tap_index]
        rounded = lax.optimization_barrier(filtered.astype(jnp.bfloat16))
        result = jnp.dot(table_wide, rounded.astype(jnp.float32).T, precision=lax.Precision.HIGHEST)
        return result.astype(jnp.bfloat16)
    spectrum = lax.map(channelize, inputs)
    spectrum = spectrum.reshape(2 * TILES, 2, FINE, SPECTRA)
    row_ids = jnp.arange(2 * TILES, dtype=jnp.int32)
    upper = row_ids[None, :] >= row_ids[:, None]

    def correlate(channel_index):
        picked = lax.dynamic_index_in_dim(spectrum, channel_index, 2, keepdims=False).astype(jnp.float32)
        real_part = picked[:, 0, :]
        imag_part = picked[:, 1, :]
        real_gram = (jnp.dot(real_part, real_part.T, precision=lax.Precision.HIGHEST) + jnp.dot(imag_part, imag_part.T, precision=lax.Precision.HIGHEST)) * jnp.float32(1.0 / SPECTRA)
        imag_gram = (jnp.dot(imag_part, real_part.T, precision=lax.Precision.HIGHEST) - jnp.dot(real_part, imag_part.T, precision=lax.Precision.HIGHEST)) * jnp.float32(1.0 / SPECTRA)
        return jnp.where(upper, real_gram, imag_gram)
    packed = lax.map(correlate, jnp.arange(FINE, dtype=jnp.int32))
    return packed.reshape(FINE, 2, TILES, 2 * TILES)
```

```python
import functools
import math

import jax
import jax.numpy as jnp
import numpy as np
from jax import lax
from jax.experimental import pallas as pl
from jax.experimental.pallas import tpu as pltpu
from jax.sharding import PartitionSpec as P

MESH = pl.DeviceIdType.MESH
LANES = 128


def phase_table(points, owners):
    column = np.arange(points)
    channel = np.arange(points // 2)
    angles = ((channel[:, None] * column[None, :]) % points).astype(np.float32) * np.float32(
        2.0 * math.pi / points
    )
    weight = np.float32(1.0 / math.sqrt(points))
    table = np.stack([np.cos(angles) * weight, -np.sin(angles) * weight])
    table = table.reshape(2, owners, points // 2 // owners, points).transpose(1, 0, 2, 3)
    return table.reshape(owners, points // owners, points).astype(jnp.bfloat16)


def channelize_kernel(
    dims, volts, taps, table, out, frames, filtered, product, send, load_sem, own_sem, send_sem,
    recv_sem, pass_sem, passed_sem
):
    owners, steps, pieces, group, taps_count, points = dims
    half = owners // 2
    me = lax.axis_index("chan")
    core = lax.axis_index("quad")
    width = (LANES + taps_count - 1) * points

    def load(k):
        return pltpu.make_async_copy(
            volts.at[0, pl.ds((k // pieces) * group, group), pl.ds((k % pieces) * LANES * points, width)],
            frames.at[k % 2],
            load_sem.at[k % 2],
        )

    def partner(j):
        return ((me // half + 1 - j // half) % 2) * half + (me + j + j // half) % half

    def to_owner(k, d):
        return pltpu.make_async_remote_copy(
            src_ref=send.at[k, d],
            dst_ref=out.at[core, me, k],
            send_sem=send_sem.at[k, d],
            recv_sem=recv_sem.at[k, me],
            device_id={"chan": d},
            device_id_type=MESH,
        )

    def from_tile(k, c):
        return pltpu.make_async_remote_copy(
            src_ref=send.at[k, c],
            dst_ref=out.at[core, c, k],
            send_sem=send_sem.at[k, c],
            recv_sem=recv_sem.at[k, c],
            device_id={"chan": c},
            device_id_type=MESH,
        )

    def to_core(k, c, block):
        return pltpu.make_async_remote_copy(
            src_ref=block,
            dst_ref=out.at[core, c, k],
            send_sem=pass_sem.at[k, c],
            recv_sem=passed_sem.at[k, c],
            device_id={"quad": 1 - core},
            device_id_type=MESH,
        )

    def from_core(k, c):
        return pltpu.make_async_remote_copy(
            src_ref=send.at[k, c],
            dst_ref=out.at[1 - core, c, k],
            send_sem=pass_sem.at[k, c],
            recv_sem=passed_sem.at[k, c],
            device_id={"quad": 1 - core},
            device_id_type=MESH,
        )

    def keep(k):
        return pltpu.make_async_copy(send.at[k, me], out.at[core, me, k], own_sem.at[k])

    def filter_block(k):
        slot = k % 2

        def body(i, carry):
            rows = i // (points // LANES)
            lanes = pl.multiple_of((i % (points // LANES)) * LANES, LANES)
            gains = [taps[m : m + 1, pl.ds(lanes, LANES)] for m in range(taps_count)]
            parts = [
                frames[
                    slot, :, pl.ds(pl.multiple_of((rows * 16 + m) * points + lanes, LANES), LANES)
                ].astype(jnp.float32)
                for m in range(16 + taps_count - 1)
            ]
            sums = []
            for s in range(16):
                total = parts[s] * gains[0]
                for m in range(1, taps_count):
                    total = total + parts[s + m] * gains[m]
                sums.append(total)
            turned = jnp.swapaxes(jnp.stack(sums, axis=0), 0, 1).astype(jnp.bfloat16)
            filtered[:, pl.ds(pl.multiple_of(rows * 16, 16), 16), pl.ds(lanes, LANES)] = turned
            return carry

        lax.fori_loop(0, (LANES // 16) * (points // LANES), body, 0)

    def transform(k, d):
        def multiply(p, carry):
            pair = filtered[pl.ds(2 * p, 2)].reshape(2 * LANES, points)
            y = lax.dot_general(
                table[d], pair, (((1,), (1,)), ((), ())), preferred_element_type=jnp.float32
            )
            product[2 * p] = y[:, :LANES]
            product[2 * p + 1] = y[:, LANES:]
            return carry

        lax.fori_loop(0, group // 2, multiply, 0)

        def turn(r, carry):
            rows = pl.ds(pl.multiple_of(r * 16, 16), 16)
            send[k, d, rows] = jnp.swapaxes(product[:, rows, :], 0, 1).astype(jnp.bfloat16)
            return carry

        lax.fori_loop(0, points // owners // 16, turn, 0)

    barrier = pltpu.get_barrier_semaphore()
    load(0).start()

    def greet(j, carry):
        pl.semaphore_signal(barrier, inc=1, device_id={"chan": partner(j)}, device_id_type=MESH)
        return carry

    lax.fori_loop(0, owners - 1, greet, 0)
    pl.semaphore_signal(barrier, inc=1, device_id={"quad": 1 - core}, device_id_type=MESH)
    pl.semaphore_wait(barrier, owners)

    def step(k, carry):
        load(k).wait()

        @pl.when(k + 1 < steps)
        def _():
            load(k + 1).start()

        filter_block(k)

        def one(j, inner):
            d = partner(j)
            transform(k, d)
            to_owner(k, d).start()
            return inner

        lax.fori_loop(0, owners - 1, one, 0)
        transform(k, me)
        keep(k).start()
        to_core(k, me, send.at[k, me]).start()
        return carry

    lax.fori_loop(0, steps, step, 0)

    def forward(i, carry):
        k, c = i // (owners - 1), partner(i % (owners - 1))
        from_tile(k, c).wait_recv()
        to_core(k, c, out.at[core, c, k]).start()
        return carry

    lax.fori_loop(0, steps * (owners - 1), forward, 0)

    def finish(i, carry):
        k, c = i // (owners - 1), partner(i % (owners - 1))
        to_owner(k, c).wait_send()
        to_core(k, c, out.at[core, c, k]).wait_send()
        from_core(k, c).wait_recv()
        return carry

    lax.fori_loop(0, steps * (owners - 1), finish, 0)

    def finish_own(k, carry):
        keep(k).wait()
        to_core(k, me, send.at[k, me]).wait_send()
        from_core(k, me).wait_recv()
        return carry

    lax.fori_loop(0, steps, finish_own, 0)


def gram_kernel(channels, pieces, factor, core_ref, own, other, out):
    _, owners, groups, _, _, _, group, lanes = own.shape
    tiles = owners * groups * group
    core = core_ref[0]
    row = lax.broadcasted_iota(jnp.int32, (tiles, tiles), 0)
    col = lax.broadcasted_iota(jnp.int32, (tiles, tiles), 1)
    upper = col >= row

    def gram(a, b):
        return lax.dot_general(a, b, (((1,), (1,)), ((), ())), preferred_element_type=jnp.float32)

    def part(ref, f, kind):
        return jnp.concatenate(
            [ref[0, :, :, s, kind, f].reshape(tiles, lanes) for s in range(pieces)], axis=-1
        )

    for f in range(channels):
        re, im = part(own, f, 0), part(own, f, 1)
        other_re, other_im = part(other, f, 0), part(other, f, 1)
        right = jnp.concatenate([re, im], axis=-1)
        crossed = jnp.concatenate([im, -re], axis=-1)
        left = jnp.where(core == 0, right, crossed)
        mine = jnp.where(upper, gram(right, right), gram(crossed, right)) * factor
        cross = gram(left, jnp.concatenate([other_re, other_im], axis=-1)) * factor
        out[f, 0, :, pl.ds(pl.multiple_of(core * tiles, LANES), tiles)] = mine
        out[f, 0, :, pl.ds(pl.multiple_of((1 - core) * tiles, LANES), tiles)] = cross


def on_device(owners, voltages, filter_taps):
    tile_count = voltages.shape[1]
    taps_count, points = filter_taps.shape
    spectra = voltages.shape[2] // points - taps_count + 1
    group = min(16, tile_count)
    groups, pieces = tile_count // group, spectra // LANES
    steps = groups * pieces
    rows = points // owners
    fine = rows // 2
    exchanged = pl.pallas_call(
        functools.partial(
            channelize_kernel, (owners, steps, pieces, group, taps_count, points)
        ),
        out_shape=jax.ShapeDtypeStruct((2, owners, steps, rows, group, LANES), jnp.bfloat16),
        in_specs=[
            pl.BlockSpec(memory_space=pl.ANY),
            pl.BlockSpec(memory_space=pltpu.VMEM),
            pl.BlockSpec(memory_space=pltpu.VMEM),
        ],
        out_specs=pl.BlockSpec(memory_space=pl.ANY),
        scratch_shapes=[
            pltpu.VMEM((2, group, (LANES + taps_count - 1) * points), jnp.bfloat16),
            pltpu.VMEM((group, LANES, points), jnp.bfloat16),
            pltpu.VMEM((group, rows, LANES), jnp.float32),
            pltpu.VMEM((steps, owners, rows, group, LANES), jnp.bfloat16),
            pltpu.SemaphoreType.DMA((2,)),
            pltpu.SemaphoreType.DMA((steps,)),
            pltpu.SemaphoreType.DMA((steps, owners)),
            pltpu.SemaphoreType.DMA((steps, owners)),
            pltpu.SemaphoreType.DMA((steps, owners)),
            pltpu.SemaphoreType.DMA((steps, owners)),
        ],
        compiler_params=pltpu.CompilerParams(
            collective_id=0, has_side_effects=True, vmem_limit_bytes=52 * 2**20
        ),
    )(voltages, filter_taps, jnp.asarray(phase_table(points, owners)))
    parts = exchanged.reshape(2, owners, groups, pieces, 2, fine, group, LANES)
    block = min(4, fine)
    tiles = owners * tile_count
    core = lax.axis_index("quad").astype(jnp.int32).reshape(1)

    def spec(which):
        return pl.BlockSpec(
            (1, owners, groups, pieces, 2, block, group, LANES),
            lambda i, c: (which(c[0]), 0, 0, 0, 0, i, 0, 0),
        )

    return pl.pallas_call(
        functools.partial(gram_kernel, block, pieces, 1.0 / spectra),
        out_shape=jax.ShapeDtypeStruct((fine, 1, tiles, 2 * tiles), jnp.float32),
        grid_spec=pltpu.PrefetchScalarGridSpec(
            num_scalar_prefetch=1,
            grid=(fine // block,),
            in_specs=[spec(lambda c: c), spec(lambda c: 1 - c)],
            out_specs=pl.BlockSpec((block, 1, tiles, 2 * tiles), lambda i, c: (i, 0, 0, 0)),
        ),
        compiler_params=pltpu.CompilerParams(vmem_limit_bytes=48 * 2**20),
    )(core, parts, parts)


def solution(mesh):
    placed = (P(("groups", "quad"), "chan", None), P())
    return jax.shard_map(
        functools.partial(on_device, mesh.shape["chan"]),
        mesh=mesh,
        in_specs=placed,
        out_specs=P(("groups", "chan"), "quad", None, None),
        check_vma=False,
    )
```

```python
import functools
import math

import jax
import jax.numpy as jnp
import numpy as np
from jax import lax
from jax.experimental import pallas as pl
from jax.experimental.pallas import tpu as pltpu
from jax.sharding import PartitionSpec as P

MESH = pl.DeviceIdType.MESH
LANES = 128


def phase_table(points, owners):
    column = np.arange(points)
    channel = np.arange(points // 2)
    angles = ((channel[:, None] * column[None, :]) % points).astype(np.float32) * np.float32(
        2.0 * math.pi / points
    )
    weight = np.float32(1.0 / math.sqrt(points))
    table = np.stack([np.cos(angles) * weight, -np.sin(angles) * weight])
    table = table.reshape(2, owners, points // 2 // owners, points).transpose(1, 0, 2, 3)
    return table.reshape(owners, points // owners, points).astype(jnp.bfloat16)


def channelize_kernel(
    dims, volts, taps, table, out, frames, filtered, product, send, load_sem, own_sem, send_sem,
    recv_sem, pass_sem, passed_sem
):
    owners, steps, pieces, group, taps_count, points = dims
    me = lax.axis_index("chan")
    core = lax.axis_index("quad")
    width = (LANES + taps_count - 1) * points

    def load(k):
        return pltpu.make_async_copy(
            volts.at[0, pl.ds((k // pieces) * group, group), pl.ds((k % pieces) * LANES * points, width)],
            frames.at[k % 2],
            load_sem.at[k % 2],
        )

    def partner(j):
        return (me + 1 + j) % owners

    def to_owner(k, d):
        return pltpu.make_async_remote_copy(
            src_ref=send.at[k, d],
            dst_ref=out.at[core, me, k],
            send_sem=send_sem.at[k, d],
            recv_sem=recv_sem.at[k, me],
            device_id={"chan": d},
            device_id_type=MESH,
        )

    def from_tile(k, c):
        return pltpu.make_async_remote_copy(
            src_ref=send.at[k, c],
            dst_ref=out.at[core, c, k],
            send_sem=send_sem.at[k, c],
            recv_sem=recv_sem.at[k, c],
            device_id={"chan": c},
            device_id_type=MESH,
        )

    def to_core(k, c, block):
        return pltpu.make_async_remote_copy(
            src_ref=block,
            dst_ref=out.at[core, c, k],
            send_sem=pass_sem.at[k, c],
            recv_sem=passed_sem.at[k, c],
            device_id={"quad": 1 - core},
            device_id_type=MESH,
        )

    def from_core(k, c):
        return pltpu.make_async_remote_copy(
            src_ref=send.at[k, c],
            dst_ref=out.at[1 - core, c, k],
            send_sem=pass_sem.at[k, c],
            recv_sem=passed_sem.at[k, c],
            device_id={"quad": 1 - core},
            device_id_type=MESH,
        )

    def keep(k):
        return pltpu.make_async_copy(send.at[k, me], out.at[core, me, k], own_sem.at[k])

    def filter_block(k):
        slot = k % 2

        def body(i, carry):
            rows = i // (points // LANES)
            lanes = pl.multiple_of((i % (points // LANES)) * LANES, LANES)
            gains = [taps[m : m + 1, pl.ds(lanes, LANES)] for m in range(taps_count)]
            parts = [
                frames[
                    slot, :, pl.ds(pl.multiple_of((rows * 16 + m) * points + lanes, LANES), LANES)
                ].astype(jnp.float32)
                for m in range(16 + taps_count - 1)
            ]
            sums = []
            for s in range(16):
                total = parts[s] * gains[0]
                for m in range(1, taps_count):
                    total = total + parts[s + m] * gains[m]
                sums.append(total)
            turned = jnp.swapaxes(jnp.stack(sums, axis=0), 0, 1).astype(jnp.bfloat16)
            filtered[:, pl.ds(pl.multiple_of(rows * 16, 16), 16), pl.ds(lanes, LANES)] = turned
            return carry

        lax.fori_loop(0, (LANES // 16) * (points // LANES), body, 0)

    def transform(k, d):
        def multiply(p, carry):
            pair = filtered[pl.ds(2 * p, 2)].reshape(2 * LANES, points)
            y = lax.dot_general(
                table[d], pair, (((1,), (1,)), ((), ())), preferred_element_type=jnp.float32
            )
            product[2 * p] = y[:, :LANES]
            product[2 * p + 1] = y[:, LANES:]
            return carry

        lax.fori_loop(0, group // 2, multiply, 0, unroll=True)

        def turn(r, carry):
            rows = pl.ds(pl.multiple_of(r * 16, 16), 16)
            send[k, d, rows] = jnp.swapaxes(product[:, rows, :], 0, 1).astype(jnp.bfloat16)
            return carry

        lax.fori_loop(0, points // owners // 16, turn, 0, unroll=True)

    barrier = pltpu.get_barrier_semaphore()
    load(0).start()

    def greet(j, carry):
        pl.semaphore_signal(barrier, inc=1, device_id={"chan": partner(j)}, device_id_type=MESH)
        return carry

    lax.fori_loop(0, owners - 1, greet, 0)
    pl.semaphore_signal(barrier, inc=1, device_id={"quad": 1 - core}, device_id_type=MESH)
    pl.semaphore_wait(barrier, owners)

    def step(k, carry):
        load(k).wait()

        @pl.when(k + 1 < steps)
        def _():
            load(k + 1).start()

        filter_block(k)

        def one(j, inner):
            d = partner(j)
            transform(k, d)
            to_owner(k, d).start()
            return inner

        lax.fori_loop(0, owners - 1, one, 0)
        transform(k, me)
        keep(k).start()
        to_core(k, me, send.at[k, me]).start()
        return carry

    lax.fori_loop(0, steps, step, 0)

    def forward(i, carry):
        k, c = i // (owners - 1), partner(i % (owners - 1))
        from_tile(k, c).wait_recv()
        to_core(k, c, out.at[core, c, k]).start()
        return carry

    lax.fori_loop(0, steps * (owners - 1), forward, 0)

    def finish(i, carry):
        k, c = i // (owners - 1), partner(i % (owners - 1))
        to_owner(k, c).wait_send()
        to_core(k, c, out.at[core, c, k]).wait_send()
        from_core(k, c).wait_recv()
        return carry

    lax.fori_loop(0, steps * (owners - 1), finish, 0)

    def finish_own(k, carry):
        keep(k).wait()
        to_core(k, me, send.at[k, me]).wait_send()
        from_core(k, me).wait_recv()
        return carry

    lax.fori_loop(0, steps, finish_own, 0)


def gram_kernel(channels, pieces, factor, core_ref, own, other, out):
    _, owners, groups, _, _, _, group, lanes = own.shape
    tiles = owners * groups * group
    core = core_ref[0]
    row = lax.broadcasted_iota(jnp.int32, (tiles, tiles), 0)
    col = lax.broadcasted_iota(jnp.int32, (tiles, tiles), 1)
    upper = col >= row

    def gram(a, b):
        return lax.dot_general(a, b, (((1,), (1,)), ((), ())), preferred_element_type=jnp.float32)

    def part(ref, f, kind):
        return jnp.concatenate(
            [ref[0, :, :, s, kind, f].reshape(tiles, lanes) for s in range(pieces)], axis=-1
        )

    for f in range(channels):
        re, im = part(own, f, 0), part(own, f, 1)
        other_re, other_im = part(other, f, 0), part(other, f, 1)
        right = jnp.concatenate([re, im], axis=-1)
        crossed = jnp.concatenate([im, -re], axis=-1)
        left = jnp.where(core == 0, right, crossed)
        mine = jnp.where(upper, gram(right, right), gram(crossed, right)) * factor
        cross = gram(left, jnp.concatenate([other_re, other_im], axis=-1)) * factor
        out[f, 0, :, pl.ds(pl.multiple_of(core * tiles, LANES), tiles)] = mine
        out[f, 0, :, pl.ds(pl.multiple_of((1 - core) * tiles, LANES), tiles)] = cross


def on_device(owners, voltages, filter_taps):
    tile_count = voltages.shape[1]
    taps_count, points = filter_taps.shape
    spectra = voltages.shape[2] // points - taps_count + 1
    group = min(16, tile_count)
    groups, pieces = tile_count // group, spectra // LANES
    steps = groups * pieces
    rows = points // owners
    fine = rows // 2
    exchanged = pl.pallas_call(
        functools.partial(
            channelize_kernel, (owners, steps, pieces, group, taps_count, points)
        ),
        out_shape=jax.ShapeDtypeStruct((2, owners, steps, rows, group, LANES), jnp.bfloat16),
        in_specs=[
            pl.BlockSpec(memory_space=pl.ANY),
            pl.BlockSpec(memory_space=pltpu.VMEM),
            pl.BlockSpec(memory_space=pltpu.VMEM),
        ],
        out_specs=pl.BlockSpec(memory_space=pl.ANY),
        scratch_shapes=[
            pltpu.VMEM((2, group, (LANES + taps_count - 1) * points), jnp.bfloat16),
            pltpu.VMEM((group, LANES, points), jnp.bfloat16),
            pltpu.VMEM((group, rows, LANES), jnp.float32),
            pltpu.VMEM((steps, owners, rows, group, LANES), jnp.bfloat16),
            pltpu.SemaphoreType.DMA((2,)),
            pltpu.SemaphoreType.DMA((steps,)),
            pltpu.SemaphoreType.DMA((steps, owners)),
            pltpu.SemaphoreType.DMA((steps, owners)),
            pltpu.SemaphoreType.DMA((steps, owners)),
            pltpu.SemaphoreType.DMA((steps, owners)),
        ],
        compiler_params=pltpu.CompilerParams(
            collective_id=0, has_side_effects=True, vmem_limit_bytes=52 * 2**20
        ),
    )(voltages, filter_taps, jnp.asarray(phase_table(points, owners)))
    parts = exchanged.reshape(2, owners, groups, pieces, 2, fine, group, LANES)
    block = min(16, fine)
    tiles = owners * tile_count
    core = lax.axis_index("quad").astype(jnp.int32).reshape(1)

    def spec(which):
        return pl.BlockSpec(
            (1, owners, groups, pieces, 2, block, group, LANES),
            lambda i, c: (which(c[0]), 0, 0, 0, 0, i, 0, 0),
        )

    return pl.pallas_call(
        functools.partial(gram_kernel, block, pieces, 1.0 / spectra),
        out_shape=jax.ShapeDtypeStruct((fine, 1, tiles, 2 * tiles), jnp.float32),
        grid_spec=pltpu.PrefetchScalarGridSpec(
            num_scalar_prefetch=1,
            grid=(fine // block,),
            in_specs=[spec(lambda c: c), spec(lambda c: 1 - c)],
            out_specs=pl.BlockSpec((block, 1, tiles, 2 * tiles), lambda i, c: (i, 0, 0, 0)),
        ),
        compiler_params=pltpu.CompilerParams(vmem_limit_bytes=48 * 2**20),
    )(core, parts, parts)


def solution(mesh):
    placed = (P(("groups", "quad"), "chan", None), P())
    return jax.shard_map(
        functools.partial(on_device, mesh.shape["chan"]),
        mesh=mesh,
        in_specs=placed,
        out_specs=P(("groups", "chan"), "quad", None, None),
        check_vma=False,
    )
```

```python
import functools
import math

import jax
import jax.numpy as jnp
import numpy as np
from jax import lax
from jax.experimental import pallas as pl
from jax.experimental.pallas import tpu as pltpu
from jax.sharding import PartitionSpec as P

MESH = pl.DeviceIdType.MESH
LANES = 128


def phase_table(points, owners):
    column = np.arange(points)
    channel = np.arange(points // 2)
    angles = ((channel[:, None] * column[None, :]) % points).astype(np.float32) * np.float32(
        2.0 * math.pi / points
    )
    weight = np.float32(1.0 / math.sqrt(points))
    table = np.stack([np.cos(angles) * weight, -np.sin(angles) * weight])
    table = table.reshape(2, owners, points // 2 // owners, points).transpose(1, 0, 2, 3)
    return table.reshape(owners, points // owners, points).astype(jnp.bfloat16)


def channelize_kernel(
    dims, volts, taps, table, out, frames, filtered, product, send, load_sem, own_sem, send_sem,
    recv_sem, pass_sem, passed_sem
):
    owners, steps, pieces, group, taps_count, points = dims
    me = lax.axis_index("chan")
    core = lax.axis_index("quad")
    width = (LANES + taps_count - 1) * points

    def load(k):
        return pltpu.make_async_copy(
            volts.at[0, pl.ds((k // pieces) * group, group), pl.ds((k % pieces) * LANES * points, width)],
            frames.at[k % 2],
            load_sem.at[k % 2],
        )

    turn_way = 1 - 2 * core

    def partner(j):
        return (me + owners + (1 + j) * turn_way) % owners

    def source(j):
        return (me + owners - (1 + j) * turn_way) % owners

    def to_owner(k, d):
        return pltpu.make_async_remote_copy(
            src_ref=send.at[k, d],
            dst_ref=out.at[core, me, k],
            send_sem=send_sem.at[k, d],
            recv_sem=recv_sem.at[k, me],
            device_id={"chan": d},
            device_id_type=MESH,
        )

    def from_tile(k, c):
        return pltpu.make_async_remote_copy(
            src_ref=send.at[k, c],
            dst_ref=out.at[core, c, k],
            send_sem=send_sem.at[k, c],
            recv_sem=recv_sem.at[k, c],
            device_id={"chan": c},
            device_id_type=MESH,
        )

    def to_core(k, c, block):
        return pltpu.make_async_remote_copy(
            src_ref=block,
            dst_ref=out.at[core, c, k],
            send_sem=pass_sem.at[k, c],
            recv_sem=passed_sem.at[k, c],
            device_id={"quad": 1 - core},
            device_id_type=MESH,
        )

    def from_core(k, c):
        return pltpu.make_async_remote_copy(
            src_ref=send.at[k, c],
            dst_ref=out.at[1 - core, c, k],
            send_sem=pass_sem.at[k, c],
            recv_sem=passed_sem.at[k, c],
            device_id={"quad": 1 - core},
            device_id_type=MESH,
        )

    def keep(k):
        return pltpu.make_async_copy(send.at[k, me], out.at[core, me, k], own_sem.at[k])

    def filter_block(k):
        slot = k % 2

        def body(i, carry):
            rows = i // (points // LANES)
            lanes = pl.multiple_of((i % (points // LANES)) * LANES, LANES)
            gains = [taps[m : m + 1, pl.ds(lanes, LANES)] for m in range(taps_count)]
            parts = [
                frames[
                    slot, :, pl.ds(pl.multiple_of((rows * 16 + m) * points + lanes, LANES), LANES)
                ].astype(jnp.float32)
                for m in range(16 + taps_count - 1)
            ]
            sums = []
            for s in range(16):
                total = parts[s] * gains[0]
                for m in range(1, taps_count):
                    total = total + parts[s + m] * gains[m]
                sums.append(total)
            turned = jnp.swapaxes(jnp.stack(sums, axis=0), 0, 1).astype(jnp.bfloat16)
            filtered[:, pl.ds(pl.multiple_of(rows * 16, 16), 16), pl.ds(lanes, LANES)] = turned
            return carry

        lax.fori_loop(0, (LANES // 16) * (points // LANES), body, 0)

    def transform(k, d):
        def multiply(p, carry):
            pair = filtered[pl.ds(2 * p, 2)].reshape(2 * LANES, points)
            y = lax.dot_general(
                table[d], pair, (((1,), (1,)), ((), ())), preferred_element_type=jnp.float32
            )
            product[2 * p] = y[:, :LANES]
            product[2 * p + 1] = y[:, LANES:]
            return carry

        lax.fori_loop(0, group // 2, multiply, 0, unroll=True)

        def turn(r, carry):
            rows = pl.ds(pl.multiple_of(r * 16, 16), 16)
            send[k, d, rows] = jnp.swapaxes(product[:, rows, :], 0, 1).astype(jnp.bfloat16)
            return carry

        lax.fori_loop(0, points // owners // 16, turn, 0, unroll=True)

    barrier = pltpu.get_barrier_semaphore()
    load(0).start()

    def greet(j, carry):
        pl.semaphore_signal(barrier, inc=1, device_id={"chan": partner(j)}, device_id_type=MESH)
        return carry

    lax.fori_loop(0, owners - 1, greet, 0)
    pl.semaphore_signal(barrier, inc=1, device_id={"quad": 1 - core}, device_id_type=MESH)
    pl.semaphore_wait(barrier, owners)

    def step(k, carry):
        load(k).wait()

        @pl.when(k + 1 < steps)
        def _():
            load(k + 1).start()

        filter_block(k)

        def one(j, inner):
            d = partner(j)
            transform(k, d)
            to_owner(k, d).start()
            return inner

        lax.fori_loop(0, owners - 1, one, 0)
        transform(k, me)
        keep(k).start()
        to_core(k, me, send.at[k, me]).start()
        return carry

    lax.fori_loop(0, steps, step, 0)

    def forward(i, carry):
        k, c = i // (owners - 1), source(i % (owners - 1))
        from_tile(k, c).wait_recv()
        to_core(k, c, out.at[core, c, k]).start()
        return carry

    lax.fori_loop(0, steps * (owners - 1), forward, 0)

    def finish(i, carry):
        k, c = i // (owners - 1), partner(i % (owners - 1))
        to_owner(k, c).wait_send()
        to_core(k, c, out.at[core, c, k]).wait_send()
        from_core(k, c).wait_recv()
        return carry

    lax.fori_loop(0, steps * (owners - 1), finish, 0)

    def finish_own(k, carry):
        keep(k).wait()
        to_core(k, me, send.at[k, me]).wait_send()
        from_core(k, me).wait_recv()
        return carry

    lax.fori_loop(0, steps, finish_own, 0)


def gram_kernel(channels, pieces, factor, core_ref, own, other, out):
    _, owners, groups, _, _, _, group, lanes = own.shape
    tiles = owners * groups * group
    core = core_ref[0]
    row = lax.broadcasted_iota(jnp.int32, (tiles, tiles), 0)
    col = lax.broadcasted_iota(jnp.int32, (tiles, tiles), 1)
    upper = col >= row

    def gram(a, b):
        return lax.dot_general(a, b, (((1,), (1,)), ((), ())), preferred_element_type=jnp.float32)

    def part(ref, f, kind):
        return jnp.concatenate(
            [ref[0, :, :, s, kind, f].reshape(tiles, lanes) for s in range(pieces)], axis=-1
        )

    for f in range(channels):
        re, im = part(own, f, 0), part(own, f, 1)
        other_re, other_im = part(other, f, 0), part(other, f, 1)
        right = jnp.concatenate([re, im], axis=-1)
        crossed = jnp.concatenate([im, -re], axis=-1)
        left = jnp.where(core == 0, right, crossed)
        mine = jnp.where(upper, gram(right, right), gram(crossed, right)) * factor
        cross = gram(left, jnp.concatenate([other_re, other_im], axis=-1)) * factor
        out[f, 0, :, pl.ds(pl.multiple_of(core * tiles, LANES), tiles)] = mine
        out[f, 0, :, pl.ds(pl.multiple_of((1 - core) * tiles, LANES), tiles)] = cross


def on_device(owners, voltages, filter_taps):
    tile_count = voltages.shape[1]
    taps_count, points = filter_taps.shape
    spectra = voltages.shape[2] // points - taps_count + 1
    group = min(16, tile_count)
    groups, pieces = tile_count // group, spectra // LANES
    steps = groups * pieces
    rows = points // owners
    fine = rows // 2
    exchanged = pl.pallas_call(
        functools.partial(
            channelize_kernel, (owners, steps, pieces, group, taps_count, points)
        ),
        out_shape=jax.ShapeDtypeStruct((2, owners, steps, rows, group, LANES), jnp.bfloat16),
        in_specs=[
            pl.BlockSpec(memory_space=pl.ANY),
            pl.BlockSpec(memory_space=pltpu.VMEM),
            pl.BlockSpec(memory_space=pltpu.VMEM),
        ],
        out_specs=pl.BlockSpec(memory_space=pl.ANY),
        scratch_shapes=[
            pltpu.VMEM((2, group, (LANES + taps_count - 1) * points), jnp.bfloat16),
            pltpu.VMEM((group, LANES, points), jnp.bfloat16),
            pltpu.VMEM((group, rows, LANES), jnp.float32),
            pltpu.VMEM((steps, owners, rows, group, LANES), jnp.bfloat16),
            pltpu.SemaphoreType.DMA((2,)),
            pltpu.SemaphoreType.DMA((steps,)),
            pltpu.SemaphoreType.DMA((steps, owners)),
            pltpu.SemaphoreType.DMA((steps, owners)),
            pltpu.SemaphoreType.DMA((steps, owners)),
            pltpu.SemaphoreType.DMA((steps, owners)),
        ],
        compiler_params=pltpu.CompilerParams(
            collective_id=0, has_side_effects=True, vmem_limit_bytes=52 * 2**20
        ),
    )(voltages, filter_taps, jnp.asarray(phase_table(points, owners)))
    parts = exchanged.reshape(2, owners, groups, pieces, 2, fine, group, LANES)
    block = min(16, fine)
    tiles = owners * tile_count
    core = lax.axis_index("quad").astype(jnp.int32).reshape(1)

    def spec(which):
        return pl.BlockSpec(
            (1, owners, groups, pieces, 2, block, group, LANES),
            lambda i, c: (which(c[0]), 0, 0, 0, 0, i, 0, 0),
        )

    return pl.pallas_call(
        functools.partial(gram_kernel, block, pieces, 1.0 / spectra),
        out_shape=jax.ShapeDtypeStruct((fine, 1, tiles, 2 * tiles), jnp.float32),
        grid_spec=pltpu.PrefetchScalarGridSpec(
            num_scalar_prefetch=1,
            grid=(fine // block,),
            in_specs=[spec(lambda c: c), spec(lambda c: 1 - c)],
            out_specs=pl.BlockSpec((block, 1, tiles, 2 * tiles), lambda i, c: (i, 0, 0, 0)),
        ),
        compiler_params=pltpu.CompilerParams(vmem_limit_bytes=48 * 2**20),
    )(core, parts, parts)


def solution(mesh):
    placed = (P(("groups", "quad"), "chan", None), P())
    return jax.shard_map(
        functools.partial(on_device, mesh.shape["chan"]),
        mesh=mesh,
        in_specs=placed,
        out_specs=P(("groups", "chan"), "quad", None, None),
        check_vma=False,
    )
```
